128 devices in a mesh: cache: 16 (over z, y), seq: 8 (over x, core).
Axes of the slice: x: 4, y: 4, z: 4, core: 2. Of those that a mesh axis runs over, the one named last changes fastest.
Arguments:
- kv_store: bfloat16 [128, 512, 1024], P('cache', 'seq'), may hold values from -6 to 6
- span_slot: int32 [128], replicated, may hold values from 0 to 127, as said below
- retrieval: int32 [16, 8], P('cache'), may hold values from 0 to 127, as said below
- recompute: int32 [16, 8, 77], P('cache'), may hold values from 0 to 511, as said below
- fresh_kv: bfloat16 [16, 8, 77, 1024], P('cache'), may hold values from -6 to 6
- queries: bfloat16 [16, 1536, 4096], P('cache', 'seq'), may hold values from -128 to 128
- question_kv: bfloat16 [16, 1536, 1024], P('cache', 'seq'), may hold values from -6 to 6
Outputs:
- attended: bfloat16 [16, 1536, 4096], P('cache', 'seq')
The draws below stay inside these ranges and needn't reach their ends.
Inputs may be any that keep to these rules, and one draw needn't show every extreme that they name: `span_slot`: a permutation: each slot holds exactly one span id; owner o holds slots o * 8 to (o + 1) * 8 - 1. `retrieval`: the ids of one request are distinct; at most 2 of them lie in one owner's slots, and in every request some owner holds exactly 2. `recompute`: the positions of one span of one request are distinct.
All inputs are finite; a program needn't handle non-finite values.
Results may differ from the reference program's by a relative error of at most 0.003.
Values may be sent and summed in bfloat16 or wider, within the bound.
A program may use at most 192 MiB of HBM per device.

```python
import jax
import jax.numpy as jnp
from jax import lax

HD = 128
KVH = 4
GROUP = 8
SPAN = 512
RECOMP = 77
CPR = 8
SL_DEV = 8
MOST = 2
REQS = 16
SLOTS = 128
QLEN = 1536


def routing(key):
    key_list = jax.random.split(key, 5)
    span_slot = jax.random.permutation(key_list[0], SLOTS).astype(jnp.int32)
    owner_total = SLOTS // SL_DEV
    hottest = jax.random.randint(key_list[1], (), 0, owner_total, dtype=jnp.int32)
    others = jax.vmap(lambda single: jax.random.permutation(single, owner_total - 1).astype(jnp.int32))(jax.random.split(key_list[2], REQS))
    others = (hottest + 1 + others) % owner_total
    spread = jnp.arange(CPR - MOST, dtype=jnp.int32)
    rest_owner = others[:, spread % (owner_total - 1)]
    rest_rank = jnp.broadcast_to(spread // (owner_total - 1), (REQS, CPR - MOST))
    owner_all = jnp.concatenate([jnp.full((REQS, MOST), hottest, dtype=jnp.int32), rest_owner], axis=1)
    rank_all = jnp.concatenate([jnp.broadcast_to(jnp.arange(MOST, dtype=jnp.int32), (REQS, MOST)), rest_rank], axis=1)
    offsets = jax.random.randint(key_list[3], (REQS, owner_total), 0, SL_DEV, dtype=jnp.int32)
    local_slot = (jnp.take_along_axis(offsets, owner_all, axis=1) + rank_all) % SL_DEV
    slot_ids = owner_all * SL_DEV + local_slot
    shuffle = jax.vmap(lambda single: jax.random.permutation(single, CPR).astype(jnp.int32))(jax.random.split(key_list[4], REQS))
    slot_ids = jnp.take_along_axis(slot_ids, shuffle, axis=1)
    span_of_slot = jnp.argsort(span_slot, stable=True).astype(jnp.int32)
    return (span_slot, span_of_slot[slot_ids].astype(jnp.int32))


def question_base(key):
    key_list = jax.random.split(key, 1)
    base_rows = jax.random.truncated_normal(key_list[0], -5.0, 5.0, (REQS, QLEN, 2 * KVH * HD), jnp.float32)
    key_part = base_rows[..., :KVH * HD]
    return jnp.concatenate([key_part, base_rows[..., KVH * HD:]], axis=-1)


def draw_span_slot(key, part):
    return routing(key)[0]


def draw_retrieval(key, part):
    return routing(key)[1]


def draw_recompute(key, part):
    key = jax.random.fold_in(key, 5)
    orders = jax.vmap(lambda single: jax.random.permutation(single, SPAN).astype(jnp.int32))(jax.random.split(key, REQS * CPR))
    return orders[:, :RECOMP].reshape(REQS, CPR, RECOMP).astype(jnp.int32)


def draw_question_kv(key, part):
    key_rows = question_base(key)
    return key_rows.astype(jnp.bfloat16)


def draw_queries(key, part):
    key = jax.random.fold_in(key, 11)
    result = 2.5 * jax.random.truncated_normal(key, -4.8, 4.8, (REQS, QLEN, KVH * GROUP * HD), jnp.float32)
    return result.astype(jnp.bfloat16)


def shard_levels(own_key, dims, cuts, smallest, top_value):
    def one(axis_at, shards_of):
        heights = jax.random.uniform(jax.random.fold_in(jax.random.fold_in(own_key, 6), axis_at), (shards_of,), jnp.float32, smallest / len(cuts), top_value / len(cuts))
        return jnp.repeat(jnp.exp(heights), dims[axis_at] // shards_of).reshape((-1,) + (1,) * (len(dims) - axis_at - 1))

    loudness = one(*cuts[0])
    for cut in cuts[1:]:
        loudness = loudness * one(*cut)
    return loudness


def normal_values(rng, dims, scale, limit, cuts=(), kind=jnp.bfloat16):
    gain = shard_levels(rng, dims, cuts, -0.22, 0.18) if cuts else 1.0
    values = jax.random.normal(rng, dims, jnp.float32) * scale * gain
    return jnp.minimum(jnp.maximum(values, -limit), limit).astype(kind)


def setup_inputs(seed: int = 0) -> dict:
    key_of = jax.random.split(jax.random.key(seed), 8)
    kv_store = normal_values(key_of[0], (SLOTS, SPAN, 2 * KVH * HD), 1.0, 6.0, ((0, 16), (1, 8)))
    span_slot = draw_span_slot(jax.random.fold_in(key_of[7], 71), 0)
    retrieval = draw_retrieval(jax.random.fold_in(key_of[7], 71), 0)
    recompute = draw_recompute(jax.random.fold_in(key_of[7], 71), 0)
    fresh_kv = normal_values(key_of[4], (REQS, CPR, RECOMP, 2 * KVH * HD), 1.0, 6.0, ((0, 16),))
    queries = draw_queries(jax.random.fold_in(key_of[7], 71), 0)
    question_kv = draw_question_kv(jax.random.fold_in(key_of[7], 71), 0)
    return dict(kv_store=kv_store, span_slot=span_slot, retrieval=retrieval, recompute=recompute, fresh_kv=fresh_kv, queries=queries, question_kv=question_kv)


masked_score = -1.0e30


def build_context(kv_store, span_slot, retrieval, recompute, fresh_kv):
    slot_ids = span_slot[retrieval]
    stored = kv_store[slot_ids]
    token_place = jnp.arange(SPAN, dtype=jnp.int32)
    replace_mask = recompute[:, :, None, :] == token_place[None, None, :, None]
    fresh_rows = jnp.einsum("rjtm,rjmf->rjtf", replace_mask.astype(jnp.float32), fresh_kv.astype(jnp.float32)).astype(jnp.bfloat16)
    return jnp.where(jnp.any(replace_mask, axis=-1)[..., None], fresh_rows, stored)


def attend_request(context, question_rows, query_rows):
    question_count = question_rows.shape[0]
    context_count = context.shape[0] * context.shape[1]
    key_rows = jnp.concatenate([context.reshape(context_count, -1), question_rows], axis=0)
    key_place = jnp.concatenate([jnp.full((context_count,), -1, dtype=jnp.int32), jnp.arange(question_count, dtype=jnp.int32)])
    visible = key_place[None, :] <= jnp.arange(question_count, dtype=jnp.int32)[:, None]
    key_width = KVH * HD
    key_heads = key_rows[:, :key_width].reshape(-1, KVH, HD).transpose(1, 0, 2)
    value_heads = key_rows[:, key_width:].reshape(-1, KVH, HD).transpose(1, 0, 2)
    query_heads = query_rows.reshape(question_count, KVH, GROUP, HD).transpose(1, 0, 2, 3)

    def one_group(group_args):
        query_block, key_block, value_block = group_args
        scores = jnp.einsum("qhd,kd->qhk", query_block.astype(jnp.float32), key_block.astype(jnp.float32)) * (HD ** -0.5)
        scores = jnp.where(visible[:, None, :], scores, masked_score)
        peak = jnp.max(scores, axis=-1, keepdims=True)
        weights = jnp.exp(scores - peak)
        totals = jnp.sum(weights, axis=-1)
        rounded = lax.optimization_barrier(weights.astype(jnp.bfloat16))
        result = jnp.einsum("qhk,kd->qhd", rounded.astype(jnp.float32), value_block.astype(jnp.float32)) / totals[..., None]
        return result.astype(jnp.bfloat16)

    attended = lax.map(one_group, (query_heads, key_heads, value_heads))
    return attended.transpose(1, 0, 2, 3).reshape(question_count, KVH * GROUP * HD)


def reference(kv_store, span_slot, retrieval, recompute, fresh_kv, queries, question_kv):
    context = build_context(kv_store, span_slot, retrieval, recompute, fresh_kv)

    def one_request(request_args):
        return attend_request(request_args[0], request_args[1], request_args[2])

    return lax.map(one_request, (context, question_kv, queries))
```

```python
import functools

import jax
import jax.numpy as jnp
from jax import lax
from jax.experimental import pallas as pl
from jax.experimental.pallas import tpu as pltpu
from jax.sharding import PartitionSpec as P

HD = 128
KVH = 4
GROUP = 8
SPANS = 8
MOST = 2
SLOTS_DEV = 8
PARTS = 2
RB = 512
LOG2E = 1.4426950408889634
SCALE = LOG2E * HD**-0.5
MASKED = -1.0e30
MESH = pl.DeviceIdType.MESH


def kernel(
    nc, ns,
    span_slot, retrieval, recompute, fresh_hbm, queries_hbm, question_hbm, store_hbm,
    out_hbm,
    *scratch,
):
    steps = KVH * PARTS
    recv = scratch[:steps]
    (send, store, fresh, query, out, ctx, ques, fresh_rows, keep, qt, acc, peak, vt, scores,
     slot_row, slot_all, slot_smem, send_slot, own_slot,
     local_sem, route_send, route_recv, route_smem, a2a_send, a2a_recv, ring_out, ring_in) = scratch[steps:]
    c = lax.axis_index("cache")
    s = lax.axis_index("seq")
    x, core = s // 2, s % 2
    right = lax.rem(x + 1, 4) * 2 + core
    left = lax.rem(x + 3, 4) * 2 + core
    far = lax.rem(x + 2, 4) * 2 + core
    sibling = x * 2 + (1 - core)
    tokens = store.shape[1]
    part = tokens // PARTS
    qlen = query.shape[0]
    rows = GROUP * qlen
    units = rows // RB

    def local(i):
        src, dst = (
            (store_hbm, store),
            (question_hbm.at[0], ques.at[s]),
            (queries_hbm.at[0], query),
            (fresh_hbm.at[0], fresh),
        )[i]
        return pltpu.make_async_copy(src, dst, local_sem.at[i])

    for i in range(4):
        local(i).start()

    lane = lax.broadcasted_iota(jnp.int32, (8, 128), 1)
    row = jnp.zeros((8, 128), jnp.int32)
    own = [span_slot[retrieval[0, j]] for j in range(SPANS)]
    for j in range(SPANS):
        row = jnp.where(lane == j, own[j], row)
        owner = own[j] // SLOTS_DEV
        rank = jnp.int32(0)
        for k in range(j):
            rank = rank + (own[k] // SLOTS_DEV == owner).astype(jnp.int32)
        own_slot[0, j] = owner
        own_slot[1, j] = jnp.minimum(rank, MOST - 1)
    slot_row[...] = row
    slot_all[c] = row

    barrier = pltpu.get_barrier_semaphore()

    def greet(d, _):
        pl.semaphore_signal(barrier, inc=1, device_id=(lax.rem(c + d, nc), s), device_id_type=MESH)
        return 0

    lax.fori_loop(1, nc, greet, 0)
    for peer in (left, right, sibling):
        pl.semaphore_signal(barrier, inc=1, device_id=(c, peer), device_id_type=MESH)
    pl.semaphore_wait(barrier, nc + 2)

    def route_copy(d):
        return pltpu.make_async_remote_copy(
            src_ref=slot_row, dst_ref=slot_all.at[c], send_sem=route_send.at[d], recv_sem=route_recv.at[d],
            device_id=(lax.rem(c + d, nc), s), device_id_type=MESH)

    def route_start(d, _):
        route_copy(d).start()
        return 0

    lax.fori_loop(1, nc, route_start, 0)

    def ring_copy(buf, b, n, source, peer, lo=None):
        at = buf.at[source]
        if lo is not None:
            half = buf.shape[1] // 2
            at = at.at[pl.ds(lo * half, half)]
        return pltpu.make_async_remote_copy(
            src_ref=at, dst_ref=at, send_sem=ring_out.at[b, n], recv_sem=ring_in.at[b, n],
            device_id=(c, peer), device_id_type=MESH)

    def other(index):
        return index // 2 * 2 + (1 - core)

    def ring_send(buf, b, n):
        source, peer, lo = (
            (s, right, None), (s, left, None), (s, sibling, None), (left, right, 0),
            (left, sibling, None), (right, left, 1), (right, sibling, None), (far, sibling, None),
        )[n]
        return ring_copy(buf, b, n, source, peer, lo)

    def ring_arrive(buf, b, n):
        source, peer, lo = (
            (left, right, None), (right, left, None), (other(s), sibling, None), (far, right, 0),
            (other(left), sibling, None), (far, left, 1), (other(right), sibling, None), (other(far), sibling, None),
        )[n]
        ring_copy(buf, b, n, source, peer, lo).wait_recv()

    def ring_first(buf, b):
        for n in (0, 1, 2):
            ring_send(buf, b, n).start()

    def ring_second(buf, b):
        for arrival, onward in ((0, (3, 4)), (1, (5, 6))):
            ring_arrive(buf, b, arrival)
            for n in onward:
                ring_send(buf, b, n).start()

    def ring_third(buf, b):
        ring_arrive(buf, b, 3)
        ring_arrive(buf, b, 5)
        ring_send(buf, b, 7).start()

    def ring_last(buf, b):
        for n in (2, 4, 6, 7):
            ring_arrive(buf, b, n)

    def ring_sent(buf, b):
        for n in range(8):
            ring_send(buf, b, n).wait_send()

    local(1).wait()
    ring_first(ques, steps)

    def route_wait(d, _):
        pltpu.make_async_remote_copy(
            src_ref=slot_row, dst_ref=slot_all.at[lax.rem(c + nc - d, nc)], send_sem=route_send.at[d],
            recv_sem=route_recv.at[d], device_id=(lax.rem(c + d, nc), s), device_id_type=MESH).wait()
        return 0

    lax.fori_loop(1, nc, route_wait, 0)
    to_smem = pltpu.make_async_copy(slot_all.at[:, 0], slot_smem, route_smem)
    to_smem.start()
    to_smem.wait()

    def route(r, _):
        count, first, second = jnp.int32(0), jnp.int32(0), jnp.int32(0)
        for j in range(SPANS):
            slot = slot_smem[r, j]
            mine = slot // SLOTS_DEV == c
            at = slot % SLOTS_DEV
            first = jnp.where(jnp.logical_and(mine, count == 0), at, first)
            second = jnp.where(jnp.logical_and(mine, count == 1), at, second)
            count = count + mine.astype(jnp.int32)
        send_slot[r, 0] = first
        send_slot[r, 1] = second
        return 0

    lax.fori_loop(0, nc, route, 0)
    local(0).wait()

    def fill(i):
        h, t = i // PARTS, i % PARTS

        def one(r, _):
            for k in range(MOST):
                at = send_slot[r, k]
                send[i, r, k, :, :HD] = store[at, t * part:(t + 1) * part, h * HD:(h + 1) * HD]
                send[i, r, k, :, HD:] = store[at, t * part:(t + 1) * part, (KVH + h) * HD:(KVH + h + 1) * HD]
            return 0

        lax.fori_loop(0, nc, one, 0)
        recv[i][c] = send[i, c]

        def start(d, _):
            to = lax.rem(c + d, nc)
            pltpu.make_async_remote_copy(
                src_ref=send.at[i, to], dst_ref=recv[i].at[c], send_sem=a2a_send.at[i], recv_sem=a2a_recv.at[i],
                device_id=(to, s), device_id_type=MESH).start()
            return 0

        lax.fori_loop(1, nc, start, 0)

    for i in range(steps):
        fill(i)

    local(3).wait()
    place = s * tokens + lax.broadcasted_iota(jnp.int32, (tokens, recompute.shape[2]), 0)
    for j in range(SPANS):
        hit = recompute[0, j:j + 1, :] == place
        picked = jnp.where(hit, 1.0, 0.0)
        fresh_rows[j] = jnp.dot(
            picked.astype(jnp.bfloat16), fresh[j], preferred_element_type=jnp.float32
        ).astype(jnp.bfloat16)
        kept = 1.0 - jnp.sum(picked, axis=1, keepdims=True)
        keep[j] = jnp.broadcast_to(kept, (tokens, HD)).astype(jnp.bfloat16)

    ring_second(ques, steps)

    local(2).wait()
    for h in range(KVH * GROUP):
        g, j = h // GROUP, h % GROUP
        qt[g, :, j * qlen:(j + 1) * qlen] = query[:, h * HD:(h + 1) * HD].astype(jnp.float32).T.astype(jnp.bfloat16)
    acc[...] = jnp.zeros_like(acc)
    peak[...] = jnp.full_like(peak, MASKED)
    vt[HD:] = jnp.ones_like(vt[HD:])
    ring_third(ques, steps)

    def choose(i):
        h, t = i // PARTS, i % PARTS
        pltpu.make_async_copy(recv[i].at[pl.ds(0, nc - 1)], recv[i].at[pl.ds(0, nc - 1)], a2a_recv.at[i]).wait()
        for j in range(SPANS):
            got = recv[i][own_slot[0, j], own_slot[1, j]]
            kept = keep[j, t * part:(t + 1) * part, :]
            fill_k = fresh_rows[j, t * part:(t + 1) * part, h * HD:(h + 1) * HD]
            fill_v = fresh_rows[j, t * part:(t + 1) * part, (KVH + h) * HD:(KVH + h + 1) * HD]
            ctx[i, s, j * part:(j + 1) * part, :HD] = got[:, :HD] * kept + fill_k
            ctx[i, s, j * part:(j + 1) * part, HD:] = got[:, HD:] * kept + fill_v
        ring_first(ctx.at[i], i)

    def attend(g, keys, values, hidden, hooks):
        count = keys.shape[0]
        vt[:HD, :count] = values.T

        def fill_scores(u):
            scores[u % 2, :count] = jnp.dot(
                keys, qt[g, :, u * RB:(u + 1) * RB], preferred_element_type=jnp.float32)

        fill_scores(0)
        for u in range(units):
            if u < len(hooks):
                hooks[u]()
            if u + 1 < units:
                fill_scores(u + 1)
            cols = slice(u * RB, (u + 1) * RB)
            score = scores[u % 2, :count]
            if hidden is not None:
                score = hidden(score, u)
            old = peak[g, :, cols]
            new = jnp.maximum(old, jnp.max(score, axis=0, keepdims=True))
            peak[g, :, cols] = new
            weight = jnp.exp2((score - new) * SCALE).astype(jnp.bfloat16)
            shrink = jnp.exp2((old - new) * SCALE)
            add = jnp.dot(vt[:, :count], weight, preferred_element_type=jnp.float32)
            acc[g, :, cols] = acc[g, :, cols] * shrink + add[:acc.shape[1]]

    ring_last(ques, steps)

    half = ns // 2

    def question_step(n, _):
        g, b = n // 2, n % 2

        @pl.when(b * half <= s)
        def _():
            block = ques.at[pl.ds(b * half, half)]
            keys = block[:, :, pl.ds(pl.multiple_of(g * HD, HD), HD)].reshape(half * qlen, HD)
            values = block[:, :, pl.ds(pl.multiple_of((KVH + g) * HD, HD), HD)].reshape(half * qlen, HD)

            def hidden(score, u):
                key_at = b * half * qlen + lax.broadcasted_iota(jnp.int32, score.shape, 0)
                col = u * RB + lax.broadcasted_iota(jnp.int32, score.shape, 1)
                return jnp.where(key_at <= s * qlen + col % qlen, score, MASKED)

            attend(g, keys, values, hidden, ())

        @pl.when(n == 2)
        def _():
            choose(0)

        @pl.when(n == 4)
        def _():
            ring_second(ctx.at[0], 0)

        @pl.when(n == 6)
        def _():
            ring_third(ctx.at[0], 0)

        return 0

    lax.fori_loop(0, 2 * KVH, question_step, 0)
    ring_last(ctx.at[0], 0)

    def context_step(i, _):
        g = i // PARTS

        def hook_first():
            for k in range(1, steps):
                @pl.when(i + 1 == k)
                def _():
                    choose(k)

        def hook_second():
            @pl.when(i + 1 < steps)
            def _():
                ring_second(ctx.at[i + 1], i + 1)

        def hook_third():
            @pl.when(i + 1 < steps)
            def _():
                ring_third(ctx.at[i + 1], i + 1)

        block = ctx.at[i]
        count = ns * SPANS * part
        keys = block[:, :, :HD].reshape(count, HD)
        values = block[:, :, HD:].reshape(count, HD)
        attend(g, keys, values, None, (hook_first, hook_second, hook_third))

        @pl.when(i % PARTS == PARTS - 1)
        def _():
            for j in range(GROUP):
                cols = slice(j * qlen, (j + 1) * qlen)
                o = acc[g, :HD, cols] / acc[g, HD:HD + 1, cols]
                out[g, :, j * HD:(j + 1) * HD] = o.T.astype(out.dtype)
            out_copy(g).start()

        @pl.when(i + 1 < steps)
        def _():
            ring_last(ctx.at[i + 1], i + 1)

        return 0

    def out_copy(g):
        return pltpu.make_async_copy(
            out.at[g], out_hbm.at[0, :, pl.ds(pl.multiple_of(g * GROUP * HD, HD), GROUP * HD)], local_sem.at[4 + g])

    lax.fori_loop(0, steps, context_step, 0)

    ring_sent(ques, steps)

    def sent(i, _):
        ring_sent(ctx.at[i], i)
        pltpu.make_async_copy(send.at[i, pl.ds(0, nc - 1)], send.at[i, pl.ds(0, nc - 1)], a2a_send.at[i]).wait()
        return 0

    lax.fori_loop(0, steps, sent, 0)
    for g in range(KVH):
        out_copy(g).wait()


def on_device(nc, ns, kv_store, span_slot, retrieval, recompute, fresh_kv, queries, question_kv):
    slots, tokens, features = kv_store.shape
    qlen = queries.shape[1]
    rows = GROUP * qlen
    steps = KVH * PARTS
    part = tokens // PARTS
    recomp = recompute.shape[2]
    bf16, f32, i32 = jnp.bfloat16, jnp.float32, jnp.int32
    dma = pltpu.SemaphoreType.DMA
    any_space = pl.BlockSpec(memory_space=pl.ANY)
    smem = pl.BlockSpec(memory_space=pltpu.SMEM)
    vmem = pl.BlockSpec(memory_space=pltpu.VMEM)
    keys = ns * SPANS * part
    scratch = [pltpu.VMEM((nc, MOST, part, 2 * HD), bf16) for _ in range(steps)] + [
        pltpu.VMEM((steps, nc, MOST, part, 2 * HD), bf16),
        pltpu.VMEM((slots, tokens, features), bf16),
        pltpu.VMEM((SPANS, recomp, features), bf16),
        pltpu.VMEM((qlen, KVH * GROUP * HD), bf16),
        pltpu.VMEM((KVH, qlen, GROUP * HD), bf16),
        pltpu.VMEM((steps, ns, SPANS * part, 2 * HD), bf16),
        pltpu.VMEM((ns, qlen, features), bf16),
        pltpu.VMEM((SPANS, tokens, features), bf16),
        pltpu.VMEM((SPANS, tokens, HD), bf16),
        pltpu.VMEM((KVH, HD, rows), bf16),
        pltpu.VMEM((KVH, HD + 8, rows), f32),
        pltpu.VMEM((KVH, 1, rows), f32),
        pltpu.VMEM((HD + 16, keys), bf16),
        pltpu.VMEM((2, keys, RB), f32),
        pltpu.VMEM((8, 128), i32),
        pltpu.VMEM((nc, 8, 128), i32),
        pltpu.SMEM((nc, 128), i32),
        pltpu.SMEM((nc, MOST), i32),
        pltpu.SMEM((2, SPANS), i32),
        dma((8,)),
        dma((nc,)),
        dma((nc,)),
        dma,
        dma((steps,)),
        dma((steps,)),
        dma((steps + 1, 8)),
        dma((steps + 1, 8)),
    ]
    return pl.pallas_call(
        functools.partial(kernel, nc, ns),
        out_shape=jax.ShapeDtypeStruct(queries.shape, queries.dtype),
        in_specs=[smem, smem, vmem, any_space, any_space, any_space, any_space],
        out_specs=any_space,
        scratch_shapes=scratch,
        compiler_params=pltpu.CompilerParams(
            collective_id=0, has_side_effects=True, vmem_limit_bytes=60 * 2**20
        ),
        name="spans_attention",
    )(span_slot, retrieval, recompute, fresh_kv, queries, question_kv, kv_store)


def solution(mesh):
    in_specs = (
        P("cache", "seq", None),
        P(),
        P("cache", None),
        P("cache", None, None),
        P("cache", None, None, None),
        P("cache", "seq", None),
        P("cache", "seq", None),
    )
    out_specs = P("cache", "seq", None)
    return jax.shard_map(
        functools.partial(on_device, mesh.shape["cache"], mesh.shape["seq"]),
        mesh=mesh, in_specs=in_specs, out_specs=out_specs, check_vma=False,
    )
```

```python
import functools

import jax
import jax.numpy as jnp
from jax import lax
from jax.experimental import pallas as pl
from jax.experimental.pallas import tpu as pltpu
from jax.sharding import PartitionSpec as P

HD = 128
KVH = 4
GROUP = 8
SPANS = 8
MOST = 2
SLOTS_DEV = 8
SLOT_BITS = 3
PARTS = 4
RB = 512
AHEAD = (14,8,2)
QUESTION_PACE = (4,7)
LOG2E = 1.4426950408889634
SCALE = LOG2E * HD**-0.5
MASKED = -1.0e30
MESH = pl.DeviceIdType.MESH


def kernel(
    nc, ns,
    span_slot, retrieval, recompute, fresh_hbm, queries_hbm, question_hbm, store_hbm,
    out_hbm,
    *scratch,
):
    steps = KVH * PARTS
    recv = scratch[:steps]
    (send, store, fresh, query, out, ctx, ques, onehot, fresh_rows, keep, qt, acc, peak, vt, scores,
     slot_row, slot_all, slot_smem, own_slot,
     local_sem, route_send, route_recv, route_smem, a2a_send, a2a_recv, ring_out, ring_in) = scratch[steps:]
    c = lax.axis_index("cache")
    s = lax.axis_index("seq")
    x, core = s // 2, s % 2

    def peer_at(me, d):
        return (me + d) & (nc - 1)

    right = lax.rem(x + 1, 4) * 2 + core
    left = lax.rem(x + 3, 4) * 2 + core
    far = lax.rem(x + 2, 4) * 2 + core
    sibling = x * 2 + (1 - core)
    tokens = store.shape[1]
    part = tokens // PARTS
    qlen = query.shape[0]
    rows = GROUP * qlen
    units = rows // RB

    barrier = pltpu.get_barrier_semaphore()
    for d in range(1, nc):
        pl.semaphore_signal(barrier, inc=1, device_id=(peer_at(c, d), s), device_id_type=MESH)
    for peer in (left, right, sibling):
        pl.semaphore_signal(barrier, inc=1, device_id=(c, peer), device_id_type=MESH)

    def local(i):
        if i < 2 * KVH:
            g, half = i // 2, i % 2
            src = question_hbm.at[0, :, pl.ds((half * KVH + g) * HD, HD)]
            dst = ques.at[g, s, :, pl.ds(half * HD, HD)]
        else:
            src, dst = ((store_hbm, store), (queries_hbm.at[0], query), (fresh_hbm, fresh))[i - 2 * KVH]
        return pltpu.make_async_copy(src, dst, local_sem.at[i])

    for i in range(2 * KVH + 3):
        local(i).start()

    lane = lax.broadcasted_iota(jnp.int32, (8, 128), 1)
    wanted = jnp.zeros((8, 128), jnp.int32)
    own = [span_slot[retrieval[0, j]] for j in range(SPANS)]
    owners = [lax.shift_right_logical(slot, SLOT_BITS) for slot in own]
    for j in range(SPANS):
        rank = jnp.int32(0)
        for k in range(j):
            rank = rank + (owners[k] == owners[j]).astype(jnp.int32)
        rank = jnp.minimum(rank, MOST - 1)
        wanted = jnp.where(lane == owners[j] + nc * rank, own[j] & (SLOTS_DEV - 1), wanted)
        own_slot[0, j] = owners[j]
        own_slot[1, j] = rank
    slot_row[...] = wanted
    slot_all[c] = wanted
    pl.semaphore_wait(barrier, nc + 2)

    def route_copy(d, at):
        return pltpu.make_async_remote_copy(
            src_ref=slot_row.at[0], dst_ref=slot_all.at[at, 0], send_sem=route_send.at[d], recv_sem=route_recv.at[d],
            device_id=(peer_at(c, d), s), device_id_type=MESH)

    for d in range(1, nc):
        route_copy(d, c).start()

    def ring_copy(buf, b, n, source, peer, lo=None):
        at = buf.at[source]
        if lo is not None:
            half = buf.shape[1] // 2
            at = at.at[pl.ds(lo * half, half)]
        return pltpu.make_async_remote_copy(
            src_ref=at, dst_ref=at, send_sem=ring_out.at[b, n], recv_sem=ring_in.at[b, n],
            device_id=(c, peer), device_id_type=MESH)

    def other(index):
        return index // 2 * 2 + (1 - core)

    def ring_send(buf, b, n):
        source, peer, lo = (
            (s, right, None), (s, left, None), (s, sibling, None), (left, right, 0),
            (left, sibling, None), (right, left, 1), (right, sibling, None), (far, sibling, None),
        )[n]
        return ring_copy(buf, b, n, source, peer, lo)

    def ring_arrive(buf, b, n):
        source, peer, lo = (
            (left, right, None), (right, left, None), (other(s), sibling, None), (far, right, 0),
            (other(left), sibling, None), (far, left, 1), (other(right), sibling, None), (other(far), sibling, None),
        )[n]
        ring_copy(buf, b, n, source, peer, lo).wait_recv()

    def ring_first(buf, b):
        for n in (0, 1, 2):
            ring_send(buf, b, n).start()

    def ring_second(buf, b):
        for arrival, onward in ((0, (3, 4)), (1, (5, 6))):
            ring_arrive(buf, b, arrival)
            for n in onward:
                ring_send(buf, b, n).start()

    def ring_third(buf, b):
        ring_arrive(buf, b, 3)
        ring_arrive(buf, b, 5)
        ring_send(buf, b, 7).start()

    def ring_last(buf, b):
        for n in (2, 4, 6, 7):
            ring_arrive(buf, b, n)

    def ring_sent(buf, b):
        for n in range(8):
            ring_send(buf, b, n).wait_send()

    for g in range(KVH):
        local(2 * g).wait()
        local(2 * g + 1).wait()
        ring_first(ques.at[g], steps + g)

    local(2 * KVH + 1).wait()
    for h in range(KVH * GROUP):
        g, j = h // GROUP, h % GROUP
        qt[g, :, j * qlen:(j + 1) * qlen] = query[:, h * HD:(h + 1) * HD].astype(jnp.float32).T.astype(jnp.bfloat16)

    local(2 * KVH + 2).wait()
    count = fresh.shape[0]
    place = recompute[0]
    spread = (
        lax.broadcasted_iota(jnp.int32, (place.shape[1], count), 1) // SPANS
        == lax.broadcasted_iota(jnp.int32, (place.shape[1], count), 0)
    ).astype(jnp.float32).astype(jnp.bfloat16)

    def spread_out(values):
        return jnp.dot(values.astype(jnp.float32).astype(jnp.bfloat16), spread, preferred_element_type=jnp.float32)

    places = spread_out(place // 16) * 16.0 + spread_out(place % 16)
    token = (s * tokens + lax.broadcasted_iota(jnp.int32, (tokens, count), 0)).astype(jnp.float32)
    span = lax.broadcasted_iota(jnp.int32, (tokens, count), 1) % SPANS
    for j in range(SPANS):
        hit = jnp.logical_and(places[j:j + 1, :] == token, span == j)
        picked = jnp.where(hit, 1.0, 0.0)
        onehot[j * tokens:(j + 1) * tokens, :] = picked.astype(jnp.bfloat16)
        kept = 1.0 - jnp.sum(picked, axis=1, keepdims=True)
        keep[j] = jnp.broadcast_to(kept, (tokens, HD)).astype(jnp.bfloat16)
    fresh_rows[...] = jnp.dot(onehot[...], fresh[...], preferred_element_type=jnp.float32).astype(
        jnp.bfloat16).reshape(fresh_rows.shape)

    acc[...] = jnp.zeros_like(acc)
    peak[...] = jnp.full_like(peak, MASKED)
    vt[HD:] = jnp.ones_like(vt[HD:])

    for d in range(1, nc):
        route_copy(d, peer_at(c, nc - d)).wait()
    to_smem = pltpu.make_async_copy(slot_all.at[:, 0], slot_smem, route_smem)
    to_smem.start()
    local(2 * KVH).wait()
    to_smem.wait()

    def fill(i):
        h, t = i // PARTS, i % PARTS

        def one(r, _):
            for k in range(MOST):
                at = slot_smem[r, c + nc * k]
                send[i, r, k, :, :HD] = store[at, t * part:(t + 1) * part, h * HD:(h + 1) * HD]
                send[i, r, k, :, HD:] = store[at, t * part:(t + 1) * part, (KVH + h) * HD:(KVH + h + 1) * HD]
            return 0

        lax.fori_loop(0, nc, one, 0)
        recv[i][c] = send[i, c]

        def start(d, _):
            to = peer_at(c, d)
            pltpu.make_async_remote_copy(
                src_ref=send.at[i, to], dst_ref=recv[i].at[c], send_sem=a2a_send.at[i], recv_sem=a2a_recv.at[i],
                device_id=(to, s), device_id_type=MESH).start()
            return 0

        lax.fori_loop(1, nc, start, 0)

    for i in range(steps):
        fill(i)

    def choose(i):
        h, t = i // PARTS, i % PARTS
        pltpu.make_async_copy(recv[i].at[pl.ds(0, nc - 1)], recv[i].at[pl.ds(0, nc - 1)], a2a_recv.at[i]).wait()
        for j in range(SPANS):
            got = recv[i][own_slot[0, j], own_slot[1, j]]
            kept = keep[j, t * part:(t + 1) * part, :]
            fill_k = fresh_rows[j, t * part:(t + 1) * part, h * HD:(h + 1) * HD]
            fill_v = fresh_rows[j, t * part:(t + 1) * part, (KVH + h) * HD:(KVH + h + 1) * HD]
            ctx[i, s, j * part:(j + 1) * part, :HD] = got[:, :HD] * kept + fill_k
            ctx[i, s, j * part:(j + 1) * part, HD:] = got[:, HD:] * kept + fill_v
        ring_first(ctx.at[i], i)

    def attend(g, keys, values, hidden, hook):
        count = keys.shape[0]
        vt[:HD, :count] = values.T

        def fill_scores(u):
            scores[u % 2, :count] = jnp.dot(
                keys, qt[g, :, u * RB:(u + 1) * RB], preferred_element_type=jnp.float32)

        fill_scores(0)
        for u in range(units):
            if hook is not None:
                hook(u)
            if u + 1 < units:
                fill_scores(u + 1)
            cols = slice(u * RB, (u + 1) * RB)
            score = scores[u % 2, :count]
            if hidden is not None:
                score = hidden(score, u)
            old = peak[g, :, cols]
            new = jnp.maximum(old, jnp.max(score, axis=0, keepdims=True))
            peak[g, :, cols] = new
            weight = jnp.exp2((score - new) * SCALE).astype(jnp.bfloat16)
            shrink = jnp.exp2((old - new) * SCALE)
            add = jnp.dot(vt[:, :count], weight, preferred_element_type=jnp.float32)
            acc[g, :, cols] = acc[g, :, cols] * shrink + add[:acc.shape[1]]

    half = ns // 2

    def second(k):
        ring_second(ctx.at[k], k)

    def third(k):
        ring_third(ctx.at[k], k)

    def question_second(g):
        ring_second(ques.at[g], steps + g)

    def question_third(g):
        ring_third(ques.at[g], steps + g)

    question_second(0)
    question_second(1)
    question_third(0)
    question_second(2)

    stages = ((third, AHEAD[2]), (second, AHEAD[1]), (choose, AHEAD[0]))
    prologue = [(0, question_third, 1), (0, question_second, 3), (2, question_third, 2), (4, question_third, 3)]
    for slot in range(-AHEAD[0], 0):
        for stage, ahead in stages:
            k = (slot + ahead) // units
            if (slot + ahead) % units == 0 and 0 <= k < steps:
                prologue.append((max(0, 2 * KVH + slot * QUESTION_PACE[0] // QUESTION_PACE[1]), stage, k))

    def question_step(n, _):
        g, b = n // 2, n % 2

        @pl.when(b == 0)
        def _():
            ring_last(ques.at[g], steps + g)

        @pl.when(b * half <= s)
        def _():
            block = ques.at[g, pl.ds(b * half, half)]
            keys = block[:, :, :HD].reshape(half * qlen, HD)
            values = block[:, :, HD:].reshape(half * qlen, HD)

            def hidden(score, u):
                key_at = b * half * qlen + lax.broadcasted_iota(jnp.int32, score.shape, 0)
                col = u * RB + lax.broadcasted_iota(jnp.int32, score.shape, 1)
                return jnp.where(key_at <= s * qlen + col % qlen, score, MASKED)

            attend(g, keys, values, hidden, None)

        for at, stage, k in prologue:
            @pl.when(n == at)
            def _():
                stage(k)

        return 0

    lax.fori_loop(0, 2 * KVH, question_step, 0)
    ring_last(ctx.at[0], 0)

    def context_step(i, _):
        g = i // PARTS

        def hook(u):
            for stage, ahead in stages:
                if (u + ahead) % units == 0:
                    later = (u + ahead) // units
                    if stage is choose:
                        for k in range(later, steps):
                            @pl.when(i + later == k)
                            def _():
                                choose(k)
                    else:
                        @pl.when(i + later < steps)
                        def _():
                            stage(i + later)

        block = ctx.at[i]
        count = ns * SPANS * part
        keys = block[:, :, :HD].reshape(count, HD)
        values = block[:, :, HD:].reshape(count, HD)
        attend(g, keys, values, None, hook)

        @pl.when(i % PARTS == PARTS - 1)
        def _():
            for j in range(GROUP):
                cols = slice(j * qlen, (j + 1) * qlen)
                o = acc[g, :HD, cols] / acc[g, HD:HD + 1, cols]
                out[g, :, j * HD:(j + 1) * HD] = o.T.astype(out.dtype)
            out_copy(g).start()

        @pl.when(i + 1 < steps)
        def _():
            ring_last(ctx.at[i + 1], i + 1)

        return 0

    def out_copy(g):
        return pltpu.make_async_copy(
            out.at[g], out_hbm.at[0, :, pl.ds(pl.multiple_of(g * GROUP * HD, HD), GROUP * HD)], local_sem.at[2 * KVH + 3 + g])

    lax.fori_loop(0, steps, context_step, 0)

    for g in range(KVH):
        ring_sent(ques.at[g], steps + g)

    def sent(i, _):
        ring_sent(ctx.at[i], i)
        pltpu.make_async_copy(send.at[i, pl.ds(0, nc - 1)], send.at[i, pl.ds(0, nc - 1)], a2a_send.at[i]).wait()
        return 0

    lax.fori_loop(0, steps, sent, 0)
    for g in range(KVH):
        out_copy(g).wait()


def on_device(nc, ns, kv_store, span_slot, retrieval, recompute, fresh_kv, queries, question_kv):
    slots, tokens, features = kv_store.shape
    qlen = queries.shape[1]
    rows = GROUP * qlen
    steps = KVH * PARTS
    part = tokens // PARTS
    recomp = recompute.shape[2]
    bf16, f32, i32 = jnp.bfloat16, jnp.float32, jnp.int32
    dma = pltpu.SemaphoreType.DMA
    any_space = pl.BlockSpec(memory_space=pl.ANY)
    smem = pl.BlockSpec(memory_space=pltpu.SMEM)
    vmem = pl.BlockSpec(memory_space=pltpu.VMEM)
    keys = ns * SPANS * part
    scratch = [pltpu.VMEM((nc, MOST, part, 2 * HD), bf16) for _ in range(steps)] + [
        pltpu.VMEM((steps, nc, MOST, part, 2 * HD), bf16),
        pltpu.VMEM((slots, tokens, features), bf16),
        pltpu.VMEM((SPANS * recomp, features), bf16),
        pltpu.VMEM((qlen, KVH * GROUP * HD), bf16),
        pltpu.VMEM((KVH, qlen, GROUP * HD), bf16),
        pltpu.VMEM((steps, ns, SPANS * part, 2 * HD), bf16),
        pltpu.VMEM((KVH, ns, qlen, 2 * HD), bf16),
        pltpu.VMEM((SPANS * tokens, SPANS * recomp), bf16),
        pltpu.VMEM((SPANS, tokens, features), bf16),
        pltpu.VMEM((SPANS, tokens, HD), bf16),
        pltpu.VMEM((KVH, HD, rows), bf16),
        pltpu.VMEM((KVH, HD + 8, rows), f32),
        pltpu.VMEM((KVH, 1, rows), f32),
        pltpu.VMEM((HD + 16, keys), bf16),
        pltpu.VMEM((2, keys, RB), f32),
        pltpu.VMEM((8, 128), i32),
        pltpu.VMEM((nc, 8, 128), i32),
        pltpu.SMEM((nc, 128), i32),
        pltpu.SMEM((2, SPANS), i32),
        dma((3 * KVH + 3,)),
        dma((nc,)),
        dma((nc,)),
        dma,
        dma((steps,)),
        dma((steps,)),
        dma((steps + KVH, 8)),
        dma((steps + KVH, 8)),
    ]
    return pl.pallas_call(
        functools.partial(kernel, nc, ns),
        out_shape=jax.ShapeDtypeStruct(queries.shape, queries.dtype),
        in_specs=[smem, smem, vmem, any_space, any_space, any_space, any_space],
        out_specs=any_space,
        scratch_shapes=scratch,
        compiler_params=pltpu.CompilerParams(
            collective_id=0, has_side_effects=True, vmem_limit_bytes=60 * 2**20
        ),
        name="spans_attention",
    )(span_slot, retrieval, recompute, fresh_kv[0].transpose(1, 0, 2).reshape(SPANS * recomp, features), queries, question_kv, kv_store)


def solution(mesh):
    in_specs = (
        P("cache", "seq", None),
        P(),
        P("cache", None),
        P("cache", None, None),
        P("cache", None, None, None),
        P("cache", "seq", None),
        P("cache", "seq", None),
    )
    out_specs = P("cache", "seq", None)
    return jax.shard_map(
        functools.partial(on_device, mesh.shape["cache"], mesh.shape["seq"]),
        mesh=mesh, in_specs=in_specs, out_specs=out_specs, check_vma=False,
    )
```
